32 devices in a mesh: row: 8 (over z, y), col: 4 (over x, core).
Axes of the slice: x: 2, y: 2, z: 4, core: 2. Of those that a mesh axis runs over, the one named last changes fastest.
Arguments:
- images: float32 [512, 768], P(('row', 'col')), may hold values from -0.21650635 to 0.21650635
- texts: float32 [512, 768], P(('row', 'col')), may hold values from -0.21650635 to 0.21650635
- log_temp: float32 [1], replicated, may hold values from 2 to 2.6
- bias: float32 [1], replicated, may hold values from -7 to -5
Outputs:
- loss: float32 [1], replicated
- d_log_temp: float32 [1], replicated
- d_bias: float32 [1], replicated
- grad_images: float32 [512, 768], P(('row', 'col'))
- grad_texts: float32 [512, 768], P(('row', 'col'))
The draws below stay inside these ranges and needn't reach their ends.
All inputs are finite; a program needn't handle non-finite values.
Results may differ from the reference program's by a relative error of at most 0.0003.
Values sent between devices are 32-bit elements; how exact they have to be, the bound alone decides.
A program may use at most 64 MiB of HBM per device.

```python
import jax
import jax.numpy as jnp
from jax import lax

D = 768
BATCH = 512


def shard_levels(stream_key, shape, pieces, smallest, top_value):
    factor_of, own = 1.0, jax.random.fold_in(stream_key, 6)
    for axis_at, parts in pieces:
        draws = jnp.exp(jax.random.uniform(jax.random.fold_in(own, axis_at), (parts,), jnp.float32, smallest / len(pieces), top_value / len(pieces)))
        factor_of = factor_of * jnp.repeat(draws, shape[axis_at] // parts).reshape([-1 if axis == axis_at else 1 for axis in range(len(shape))])
    return factor_of


def bell_draw(rng, dims, width, reach, cuts=(), kind=jnp.bfloat16):
    result = jax.random.normal(rng, dims, jnp.float32) * width
    if len(cuts) > 0:
        result = shard_levels(rng, dims, cuts, -0.22, 0.18) * result
    return jnp.clip(result, min=-reach, max=reach).astype(kind)


def setup_inputs(seed: int = 0) -> dict:
    key_of = jax.random.split(jax.random.key(seed), 5)
    images = bell_draw(key_of[0], (BATCH, D), (D ** -0.5), 0.21650635, ((0, 32),), jnp.float32)
    texts = bell_draw(key_of[1], (BATCH, D), (D ** -0.5), 0.21650635, ((0, 32),), jnp.float32)
    log_temp = jnp.clip(jax.random.uniform(key_of[2], (1,), jnp.float32, 2.0, 2.6), 2.0, 2.6)
    bias = jnp.clip(jax.random.uniform(key_of[3], (1,), jnp.float32, -7.0, -5.0), -7.0, -5.0)
    return {"images": images, "texts": texts, "log_temp": log_temp, "bias": bias}


def normalize(x):
    norm = jnp.sqrt(lax.optimization_barrier(jnp.sum(x * x, axis=1, keepdims=True)) + 1e-06)
    return x / norm

def reference(images, texts, log_temp, bias):
    unit_img, back_img = jax.vjp(normalize, images)
    unit_txt, back_txt = jax.vjp(normalize, texts)
    temp = jnp.exp(log_temp[0])
    shift = bias[0]
    total_rows = unit_img.shape[0]
    blk = min(total_rows, 1024)
    count = total_rows // blk
    columns = jnp.arange(total_rows, dtype=jnp.int32)

    def step(carry, index):
        grad_txt, loss_sum, temp_sum, bias_sum = carry
        start = (index * blk).astype(jnp.int32)
        block = lax.dynamic_slice_in_dim(unit_img, start, blk, 0)
        sim = jnp.dot(block, unit_txt.T, precision=lax.Precision.HIGHEST, preferred_element_type=jnp.float32)
        logit = temp * sim + shift
        rows = start + jnp.arange(blk, dtype=jnp.int32)
        sign = jnp.where(rows[:, None] == columns[None, :], 1.0, -1.0).astype(jnp.float32)
        pair_grad = -sign * jax.nn.sigmoid(-sign * logit)
        loss_sum = loss_sum + jnp.sum(jax.nn.softplus(-sign * logit))
        temp_sum = temp_sum + jnp.sum(pair_grad * sim)
        bias_sum = bias_sum + jnp.sum(pair_grad)
        grad_blk = temp * jnp.dot(pair_grad, unit_txt, precision=lax.Precision.HIGHEST, preferred_element_type=jnp.float32)
        grad_txt = grad_txt + temp * jnp.dot(pair_grad.T, block, precision=lax.Precision.HIGHEST, preferred_element_type=jnp.float32)
        return ((grad_txt, loss_sum, temp_sum, bias_sum), grad_blk)
    zero = jnp.zeros((), jnp.float32)
    init = (jnp.zeros(unit_txt.shape, jnp.float32), zero, zero, zero)
    (grad_txt, loss_sum, temp_sum, bias_sum), blocks = lax.scan(step, init, jnp.arange(count, dtype=jnp.int32))
    grad_img = blocks.reshape(unit_img.shape)
    grad_images = back_img(grad_img)[0]
    grad_texts = back_txt(grad_txt)[0]
    scale = jnp.float32(total_rows)
    loss = jnp.reshape(loss_sum / scale, (1,))
    d_log_temp = jnp.reshape(temp * temp_sum / scale, (1,))
    d_bias = jnp.reshape(bias_sum / scale, (1,))
    return (loss, d_log_temp, d_bias, grad_images, grad_texts)
```

```python
import functools

import jax
import jax.numpy as jnp
from jax import lax
from jax.experimental import pallas as pl
from jax.experimental.pallas import tpu as pltpu
from jax.sharding import PartitionSpec as P

MESH = pl.DeviceIdType.MESH
BF16 = jnp.bfloat16
F32 = jnp.float32


def split(x):
    hi = x.astype(BF16)
    return hi, (x - hi.astype(F32)).astype(BF16)


def dot(a, b, contract):
    return lax.dot_general(a, b, ((contract[:1], contract[1:]), ((), ())), preferred_element_type=F32)


def normalize(x):
    norm = jnp.sqrt(jnp.sum(x * x, axis=1, keepdims=True) + 1e-06)
    return x / norm, norm


def unnormalize(unit, norm, grad_unit):
    inner = jnp.sum(unit * grad_unit, axis=1, keepdims=True)
    return (grad_unit - unit * inner) / norm


def kernel(
    rows, cols, low,
    log_temp_ref, bias_ref, images_ref, texts_ref,
    grad_img_ref, grad_txt_ref, scalars_ref,
    images_at, texts_at, img_both, txt_both,
    img_all, txt_all, img_part, txt_part, img_recv, txt_recv, sums_img, sums_txt,
    send_img, recv_img, send_txt, recv_txt, send_pimg, recv_pimg, send_ptxt, recv_ptxt,
    send_s1, recv_s1, send_s2, recv_s2, load,
):
    n_img, n_txt = cols * low, rows // low
    shard, width = images_ref.shape
    row, col = lax.axis_index("row"), lax.axis_index("col")
    high, below = lax.div(row, low), lax.rem(row, low)
    g_img = below * cols + col
    g_txt = high

    loads = [
        pltpu.make_async_copy(texts_ref, texts_at, load.at[0]),
        pltpu.make_async_copy(images_ref, images_at, load.at[1]),
    ]
    for item in loads:
        item.start()

    img_peers, txt_peers = [], []
    for step in range(1, n_txt):
        slot = lax.rem(g_txt + step, n_txt)
        txt_peers.append((slot, (slot * low + below, col)))
    for step in range(1, n_img):
        slot = lax.rem(g_img + step, n_img)
        img_peers.append((slot, (high * low + lax.div(slot, cols), lax.rem(slot, cols))))

    barrier = pltpu.get_barrier_semaphore()
    for _, peer in txt_peers + img_peers:
        pl.semaphore_signal(barrier, inc=1, device_id=peer, device_id_type=MESH)

    m_txt, m_img = n_txt * shard, n_img * shard

    def keep(both, slot, offset, x):
        hi, lo = split(x)
        at = pl.multiple_of(slot * shard, shard)
        both[pl.ds(at, shard), :] = hi
        both[pl.ds(offset + at, shard), :] = lo

    loads[0].wait()
    unit_txt, norm_txt = normalize(texts_at[...])
    txt_all[g_txt] = unit_txt
    loads[1].wait()
    unit_img, norm_img = normalize(images_at[...])
    img_all[g_img] = unit_img
    pl.semaphore_wait(barrier, n_img + n_txt - 2)

    def copy(src, dst, send, recv, peer):
        return pltpu.make_async_remote_copy(
            src_ref=src, dst_ref=dst, send_sem=send, recv_sem=recv, device_id=peer, device_id_type=MESH
        )

    def gather(buf, send, recv, me, peers):
        for slot, peer in peers:
            copy(buf.at[me], buf.at[me], send.at[slot], recv.at[me], peer).start()

    def scatter(src, dst, send, recv, me, peers):
        for slot, peer in peers:
            copy(src.at[slot], dst.at[me], send.at[slot], recv.at[me], peer).start()

    def arrive(dst, send, recv, slot, peer):
        copy(dst.at[slot], dst.at[slot], send.at[slot], recv.at[slot], peer).wait_recv()

    def drain(dst, send, recv, peers):
        for slot, peer in peers:
            arrive(dst, send, recv, slot, peer)

    def sent(src, send, recv, peers):
        for slot, peer in peers:
            copy(src.at[slot], src.at[slot], send.at[slot], recv.at[slot], peer).wait_send()

    gather(txt_all, send_txt, recv_txt, g_txt, txt_peers)
    gather(img_all, send_img, recv_img, g_img, img_peers)

    keep(txt_both, g_txt, m_txt, unit_txt)
    keep(img_both, g_img, m_img, unit_img)
    temp = jnp.exp(jnp.full((1, 1), log_temp_ref[0], F32))
    shift = bias_ref[0]
    for slot, peer in img_peers:
        arrive(img_all, send_img, recv_img, slot, peer)
        keep(img_both, slot, m_img, img_all[slot])
    for slot, peer in txt_peers:
        arrive(txt_all, send_txt, recv_txt, slot, peer)
        keep(txt_both, slot, m_txt, txt_all[slot])

    prod = dot(txt_both[...], img_both[...], (1, 1))
    sim = (prod[:m_txt, :m_img] + prod[m_txt:, m_img:]) + (prod[:m_txt, m_img:] + prod[m_txt:, :m_img])
    logit = temp * sim + shift
    at = lax.broadcasted_iota(jnp.int32, (m_txt, m_img), 0) - g_txt * shard
    diagonal = (at == lax.broadcasted_iota(jnp.int32, (m_txt, m_img), 1) - g_img * shard) & (at >= 0) & (at < shard)
    sign = jnp.where(diagonal, 1.0, -1.0).astype(F32)
    margin = -sign * logit
    small = jnp.exp(-jnp.abs(margin))
    pair_grad = -sign * (jnp.where(margin >= 0, 1.0, small) / (1.0 + small))
    soft = jnp.maximum(margin, 0.0) + jnp.log1p(small)

    def total(x):
        return jnp.sum(jnp.sum(x, axis=0, keepdims=True), axis=1, keepdims=True)

    lane = lax.broadcasted_iota(jnp.int32, (8, 128), 1)
    part = jnp.where(lane == 0, total(soft), jnp.where(lane == 1, total(pair_grad * sim), total(pair_grad)))
    sums_img[g_img] = part
    gather(sums_img, send_s1, recv_s1, g_img, img_peers)

    g_hi, g_lo = split(temp * pair_grad)
    g_both = jnp.concatenate([g_hi, g_lo], axis=0)
    pt = dot(jnp.concatenate([g_both, g_both], axis=1), img_both[...], (1, 0))
    txt_part[...] = (pt[:m_txt] + pt[m_txt:]).reshape(n_txt, shard, width)
    scatter(txt_part, txt_recv, send_ptxt, recv_ptxt, g_txt, txt_peers)
    pi = dot(
        jnp.concatenate([g_hi, g_hi, g_lo, g_lo], axis=0),
        jnp.concatenate([txt_both[...], txt_both[...]], axis=0),
        (0, 0),
    )
    img_part[...] = pi.reshape(n_img, shard, width)
    scatter(img_part, img_recv, send_pimg, recv_pimg, g_img, img_peers)

    drain(sums_img, send_s1, recv_s1, img_peers)
    sums_txt[g_txt] = jnp.sum(sums_img[...], axis=0)
    gather(sums_txt, send_s2, recv_s2, g_txt, txt_peers)
    sent(txt_all, send_txt, recv_txt, txt_peers)
    sent(img_all, send_img, recv_img, img_peers)
    sent(sums_img, send_s1, recv_s1, img_peers)

    drain(txt_recv, send_ptxt, recv_ptxt, txt_peers)
    txt_recv[g_txt] = txt_part[g_txt]
    grad_txt_ref[...] = unnormalize(unit_txt, norm_txt, jnp.sum(txt_recv[...], axis=0))
    drain(img_recv, send_pimg, recv_pimg, img_peers)
    img_recv[g_img] = img_part[g_img]
    grad_img_ref[...] = unnormalize(unit_img, norm_img, jnp.sum(img_recv[...], axis=0))

    drain(sums_txt, send_s2, recv_s2, txt_peers)
    count = float(rows * cols * shard)
    final = jnp.sum(sums_txt[...], axis=0) / count
    scalars_ref[...] = jnp.where(lane == 1, temp * final, final)

    sent(txt_part, send_ptxt, recv_ptxt, txt_peers)
    sent(img_part, send_pimg, recv_pimg, img_peers)
    sent(sums_txt, send_s2, recv_s2, txt_peers)


def write_out(grad_img_ref, grad_txt_ref, scalars_ref, loss_ref, d_temp_ref, d_bias_ref, img_ref, txt_ref, sem):
    writes = [
        pltpu.make_async_copy(grad_img_ref, img_ref, sem.at[0]),
        pltpu.make_async_copy(grad_txt_ref, txt_ref, sem.at[1]),
    ]
    for item in writes:
        item.start()
    loss_ref[0] = scalars_ref[0, 0]
    d_temp_ref[0] = scalars_ref[0, 1]
    d_bias_ref[0] = scalars_ref[0, 2]
    for item in writes:
        item.wait()


def per_device(rows, cols, low, images, texts, log_temp, bias):
    shard, width = images.shape
    n_img, n_txt = cols * low, rows // low
    block = (shard, width)
    img_blocks, txt_blocks = pltpu.VMEM((n_img, *block), F32), pltpu.VMEM((n_txt, *block), F32)
    img_sems, txt_sems = pltpu.SemaphoreType.DMA((n_img,)), pltpu.SemaphoreType.DMA((n_txt,))
    vmem, smem = pl.BlockSpec(memory_space=pltpu.VMEM), pl.BlockSpec(memory_space=pltpu.SMEM)
    hbm = pl.BlockSpec(memory_space=pltpu.HBM)
    images, texts = (pltpu.with_memory_space_constraint(x, pltpu.HBM) for x in (images, texts))
    grad_img, grad_txt, scalars = pl.pallas_call(
        functools.partial(kernel, rows, cols, low),
        out_shape=[
            jax.ShapeDtypeStruct(block, F32),
            jax.ShapeDtypeStruct(block, F32),
            jax.ShapeDtypeStruct((8, 128), F32),
        ],
        in_specs=[smem, smem, hbm, hbm],
        out_specs=[vmem, vmem, vmem],
        scratch_shapes=[
            pltpu.VMEM(block, F32), pltpu.VMEM(block, F32),
            pltpu.VMEM((2 * n_img * shard, width), BF16), pltpu.VMEM((2 * n_txt * shard, width), BF16),
            img_blocks, txt_blocks, img_blocks, txt_blocks, img_blocks, txt_blocks,
            pltpu.VMEM((n_img, 8, 128), F32), pltpu.VMEM((n_txt, 8, 128), F32),
            img_sems, img_sems, txt_sems, txt_sems, img_sems, img_sems, txt_sems, txt_sems,
            img_sems, img_sems, txt_sems, txt_sems, pltpu.SemaphoreType.DMA((2,)),
        ],
        compiler_params=pltpu.CompilerParams(
            collective_id=0, has_side_effects=True, vmem_limit_bytes=48 * 1024 * 1024
        ),
        name="sigmoid_loss",
    )(log_temp, bias, images, texts)
    one = jax.ShapeDtypeStruct((1,), F32)
    return pl.pallas_call(
        write_out,
        out_shape=[one, one, one, jax.ShapeDtypeStruct(block, F32), jax.ShapeDtypeStruct(block, F32)],
        in_specs=[vmem, vmem, vmem],
        out_specs=[smem, smem, smem, hbm, hbm],
        scratch_shapes=[pltpu.SemaphoreType.DMA((2,))],
        name="write_out",
    )(grad_img, grad_txt, scalars)


def solution(mesh):
    rows, cols = mesh.shape["row"], mesh.shape["col"]
    low = 1
    while cols * low < rows // low and rows % (2 * low) == 0:
        low *= 2
    in_specs = (P(("row", "col"), None), P(("row", "col"), None), P(), P())
    out_specs = (P(), P(), P(), P(("row", "col"), None), P(("row", "col"), None))
    return jax.shard_map(
        functools.partial(per_device, rows, cols, low),
        mesh=mesh, in_specs=in_specs, out_specs=out_specs, check_vma=False,
    )
```

```python
import functools

import jax
import jax.numpy as jnp
from jax import lax
from jax.experimental import pallas as pl
from jax.experimental.pallas import tpu as pltpu
from jax.sharding import PartitionSpec as P

MESH = pl.DeviceIdType.MESH
BF16 = jnp.bfloat16
F32 = jnp.float32


def split(x):
    hi = x.astype(BF16)
    return hi, (x - hi.astype(F32)).astype(BF16)


def dot(a, b, contract):
    return lax.dot_general(a, b, ((contract[:1], contract[1:]), ((), ())), preferred_element_type=F32)


def normalize(x):
    norm = jnp.sqrt(jnp.sum(x * x, axis=1, keepdims=True) + 1e-06)
    return x / norm, norm


def unnormalize(unit, norm, grad_unit):
    inner = jnp.sum(unit * grad_unit, axis=1, keepdims=True)
    return (grad_unit - unit * inner) / norm


def kernel(
    rows, cols, low,
    log_temp_ref, bias_ref, images_ref, texts_ref,
    grad_img_ref, grad_txt_ref, scalars_ref,
    images_at, texts_at, img_both, txt_both,
    img_all, txt_all, img_part, txt_part, img_recv, txt_recv, sums_img, sums_txt,
    send_img, recv_img, send_txt, recv_txt, send_pimg, recv_pimg, send_ptxt, recv_ptxt,
    send_s1, recv_s1, send_s2, recv_s2, load,
):
    n_img, n_txt = cols * low, rows // low
    shard, width = images_ref.shape
    row, col = lax.axis_index("row"), lax.axis_index("col")
    high, below = lax.div(row, low), lax.rem(row, low)
    g_img = below * cols + col
    g_txt = high

    loads = [
        pltpu.make_async_copy(texts_ref, texts_at, load.at[0]),
        pltpu.make_async_copy(images_ref, images_at, load.at[1]),
    ]
    for item in loads:
        item.start()

    img_peers, txt_peers = [], []
    for step in range(1, n_txt):
        slot = lax.rem(g_txt + step, n_txt)
        txt_peers.append((slot, (slot * low + below, col)))
    for step in range(1, n_img):
        slot = lax.rem(g_img + step, n_img)
        img_peers.append((slot, (high * low + lax.div(slot, cols), lax.rem(slot, cols))))

    barrier = pltpu.get_barrier_semaphore()
    for _, peer in txt_peers + img_peers:
        pl.semaphore_signal(barrier, inc=1, device_id=peer, device_id_type=MESH)

    m_txt, m_img = n_txt * shard, n_img * shard

    def keep(both, slot, offset, x):
        hi, lo = split(x)
        at = pl.multiple_of(slot * shard, shard)
        both[pl.ds(at, shard), :] = hi
        both[pl.ds(offset + at, shard), :] = lo

    loads[0].wait()
    unit_txt, norm_txt = normalize(texts_at[...])
    txt_all[g_txt] = unit_txt
    loads[1].wait()
    unit_img, norm_img = normalize(images_at[...])
    img_all[g_img] = unit_img
    pl.semaphore_wait(barrier, n_img + n_txt - 2)

    def copy(src, dst, send, recv, peer):
        return pltpu.make_async_remote_copy(
            src_ref=src, dst_ref=dst, send_sem=send, recv_sem=recv, device_id=peer, device_id_type=MESH
        )

    def gather(buf, send, recv, me, peers):
        for slot, peer in peers:
            copy(buf.at[me], buf.at[me], send.at[slot], recv.at[me], peer).start()

    def scatter(src, dst, send, recv, me, peers):
        for slot, peer in peers:
            copy(src.at[slot], dst.at[me], send.at[slot], recv.at[me], peer).start()

    def arrive(dst, send, recv, slot, peer):
        copy(dst.at[slot], dst.at[slot], send.at[slot], recv.at[slot], peer).wait_recv()

    def drain(dst, send, recv, peers):
        for slot, peer in peers:
            arrive(dst, send, recv, slot, peer)

    def sent(src, send, recv, peers):
        for slot, peer in peers:
            copy(src.at[slot], src.at[slot], send.at[slot], recv.at[slot], peer).wait_send()

    gather(txt_all, send_txt, recv_txt, g_txt, txt_peers)
    gather(img_all, send_img, recv_img, g_img, img_peers)

    keep(txt_both, g_txt, m_txt, unit_txt)
    keep(img_both, g_img, m_img, unit_img)
    temp = jnp.exp(jnp.full((1, 1), log_temp_ref[0], F32))
    shift = bias_ref[0]
    for slot, peer in img_peers:
        arrive(img_all, send_img, recv_img, slot, peer)
        keep(img_both, slot, m_img, img_all[slot])
    for slot, peer in txt_peers:
        arrive(txt_all, send_txt, recv_txt, slot, peer)
        keep(txt_both, slot, m_txt, txt_all[slot])

    prod = dot(txt_both[...], img_both[...], (1, 1))
    sim = (prod[:m_txt, :m_img] + prod[m_txt:, m_img:]) + (prod[:m_txt, m_img:] + prod[m_txt:, :m_img])
    logit = temp * sim + shift
    at = lax.broadcasted_iota(jnp.int32, (m_txt, m_img), 0) - g_txt * shard
    diagonal = (at == lax.broadcasted_iota(jnp.int32, (m_txt, m_img), 1) - g_img * shard) & (at >= 0) & (at < shard)
    sign = jnp.where(diagonal, 1.0, -1.0).astype(F32)
    margin = -sign * logit
    small = jnp.exp(-jnp.abs(margin))
    pair_grad = -sign * (jnp.where(margin >= 0, 1.0, small) / (1.0 + small))

    def total(x):
        return jnp.sum(jnp.sum(x, axis=0, keepdims=True), axis=1, keepdims=True)

    g_hi, g_lo = split(temp * pair_grad)
    g_both = jnp.concatenate([g_hi, g_lo], axis=0)
    pt = dot(jnp.concatenate([g_both, g_both], axis=1), img_both[...], (1, 0))
    txt_part[...] = (pt[:m_txt] + pt[m_txt:]).reshape(n_txt, shard, width)
    scatter(txt_part, txt_recv, send_ptxt, recv_ptxt, g_txt, txt_peers)

    soft = jnp.maximum(margin, 0.0) + jnp.log1p(small)
    lane = lax.broadcasted_iota(jnp.int32, (8, 128), 1)
    part = jnp.where(lane == 0, total(soft), jnp.where(lane == 1, total(pair_grad * sim), total(pair_grad)))
    sums_img[g_img] = part
    gather(sums_img, send_s1, recv_s1, g_img, img_peers)

    pi = dot(
        jnp.concatenate([g_hi, g_hi, g_lo, g_lo], axis=0),
        jnp.concatenate([txt_both[...], txt_both[...]], axis=0),
        (0, 0),
    )
    img_part[...] = pi.reshape(n_img, shard, width)
    scatter(img_part, img_recv, send_pimg, recv_pimg, g_img, img_peers)

    drain(sums_img, send_s1, recv_s1, img_peers)
    sums_txt[g_txt] = jnp.sum(sums_img[...], axis=0)
    gather(sums_txt, send_s2, recv_s2, g_txt, txt_peers)
    sent(txt_all, send_txt, recv_txt, txt_peers)
    sent(img_all, send_img, recv_img, img_peers)
    sent(sums_img, send_s1, recv_s1, img_peers)

    grad_txt = txt_part[g_txt]
    for slot, peer in txt_peers:
        arrive(txt_recv, send_ptxt, recv_ptxt, slot, peer)
        grad_txt = grad_txt + txt_recv[slot]
    grad_txt_ref[...] = unnormalize(unit_txt, norm_txt, grad_txt)
    grad_img = img_part[g_img]
    for slot, peer in img_peers:
        arrive(img_recv, send_pimg, recv_pimg, slot, peer)
        grad_img = grad_img + img_recv[slot]
    grad_img_ref[...] = unnormalize(unit_img, norm_img, grad_img)

    drain(sums_txt, send_s2, recv_s2, txt_peers)
    count = float(rows * cols * shard)
    final = jnp.sum(sums_txt[...], axis=0) / count
    scalars_ref[...] = jnp.where(lane == 1, temp * final, final)

    sent(txt_part, send_ptxt, recv_ptxt, txt_peers)
    sent(img_part, send_pimg, recv_pimg, img_peers)
    sent(sums_txt, send_s2, recv_s2, txt_peers)


def write_out(grad_img_ref, grad_txt_ref, scalars_ref, loss_ref, d_temp_ref, d_bias_ref, img_ref, txt_ref, parts, sem):
    writes = [
        pltpu.make_async_copy(grad_img_ref, img_ref, sem.at[0]),
        pltpu.make_async_copy(grad_txt_ref, txt_ref, sem.at[1]),
    ]
    for at, ref in enumerate((loss_ref, d_temp_ref, d_bias_ref)):
        parts[at] = scalars_ref[0:1, at : at + 1]
        writes.append(pltpu.make_async_copy(parts.at[at], ref, sem.at[2 + at]))
    for item in writes:
        item.start()
    for item in writes:
        item.wait()


def per_device(rows, cols, low, images, texts, log_temp, bias):
    shard, width = images.shape
    n_img, n_txt = cols * low, rows // low
    block = (shard, width)
    img_blocks, txt_blocks = pltpu.VMEM((n_img, *block), F32), pltpu.VMEM((n_txt, *block), F32)
    img_sems, txt_sems = pltpu.SemaphoreType.DMA((n_img,)), pltpu.SemaphoreType.DMA((n_txt,))
    vmem, smem = pl.BlockSpec(memory_space=pltpu.VMEM), pl.BlockSpec(memory_space=pltpu.SMEM)
    hbm = pl.BlockSpec(memory_space=pltpu.HBM)
    images, texts = (pltpu.with_memory_space_constraint(x, pltpu.HBM) for x in (images, texts))
    grad_img, grad_txt, scalars = pl.pallas_call(
        functools.partial(kernel, rows, cols, low),
        out_shape=[
            pltpu.VMEM(block, F32),
            pltpu.VMEM(block, F32),
            pltpu.VMEM((8, 128), F32),
        ],
        in_specs=[smem, smem, hbm, hbm],
        out_specs=[vmem, vmem, vmem],
        scratch_shapes=[
            pltpu.VMEM(block, F32), pltpu.VMEM(block, F32),
            pltpu.VMEM((2 * n_img * shard, width), BF16), pltpu.VMEM((2 * n_txt * shard, width), BF16),
            img_blocks, txt_blocks, img_blocks, txt_blocks, img_blocks, txt_blocks,
            pltpu.VMEM((n_img, 8, 128), F32), pltpu.VMEM((n_txt, 8, 128), F32),
            img_sems, img_sems, txt_sems, txt_sems, img_sems, img_sems, txt_sems, txt_sems,
            img_sems, img_sems, txt_sems, txt_sems, pltpu.SemaphoreType.DMA((2,)),
        ],
        compiler_params=pltpu.CompilerParams(
            collective_id=0, has_side_effects=True, vmem_limit_bytes=48 * 1024 * 1024
        ),
        name="sigmoid_loss",
    )(log_temp, bias, images, texts)
    one = jax.ShapeDtypeStruct((1, 1), F32)
    held = (pltpu.with_memory_space_constraint(x, pltpu.VMEM) for x in (grad_img, grad_txt, scalars))
    loss, d_temp, d_bias, grad_img, grad_txt = pl.pallas_call(
        write_out,
        out_shape=[one, one, one, jax.ShapeDtypeStruct(block, F32), jax.ShapeDtypeStruct(block, F32)],
        in_specs=[vmem, vmem, vmem],
        out_specs=[hbm] * 5,
        scratch_shapes=[pltpu.VMEM((3, 1, 1), F32), pltpu.SemaphoreType.DMA((5,))],
        name="write_out",
    )(*held)
    return loss.reshape(1), d_temp.reshape(1), d_bias.reshape(1), grad_img, grad_txt


def solution(mesh):
    rows, cols = mesh.shape["row"], mesh.shape["col"]
    low = 1
    while cols * low < rows // low and rows % (2 * low) == 0:
        low *= 2
    in_specs = (P(("row", "col"), None), P(("row", "col"), None), P(), P())
    out_specs = (P(), P(), P(), P(("row", "col"), None), P(("row", "col"), None))
    return jax.shard_map(
        functools.partial(per_device, rows, cols, low),
        mesh=mesh, in_specs=in_specs, out_specs=out_specs, check_vma=False,
    )
```

```python
import functools

import jax
import jax.numpy as jnp
from jax import lax
from jax.experimental import pallas as pl
from jax.experimental.pallas import tpu as pltpu
from jax.sharding import PartitionSpec as P

MESH = pl.DeviceIdType.MESH
BF16 = jnp.bfloat16
F32 = jnp.float32


def split(x):
    hi = x.astype(BF16)
    return hi, (x - hi.astype(F32)).astype(BF16)


def dot(a, b, contract):
    return lax.dot_general(a, b, ((contract[:1], contract[1:]), ((), ())), preferred_element_type=F32)


def paired(slot, step, count):
    if count & (count - 1):
        return lax.rem(slot + step, count)
    bit = 1
    while bit < count:
        if step & bit:
            slot = slot + bit - 2 * bit * lax.rem(lax.div(slot, bit), 2)
        bit *= 2
    return slot


def normalize(x):
    norm = jnp.sqrt(jnp.sum(x * x, axis=1, keepdims=True) + 1e-06)
    return x / norm, norm


def unnormalize(unit, norm, grad_unit):
    inner = jnp.sum(unit * grad_unit, axis=1, keepdims=True)
    return (grad_unit - unit * inner) / norm


def kernel(
    rows, cols, low,
    scale_ref, images_ref, texts_ref,
    grad_img_ref, grad_txt_ref, scalars_ref,
    images_at, texts_at, img_both,
    img_all, txt_all, img_part, txt_part, img_recv, txt_recv, sums_img, sums_txt,
    send_img, recv_img, send_txt, recv_txt, send_pimg, recv_pimg, send_ptxt, recv_ptxt,
    send_s1, recv_s1, send_s2, recv_s2, load,
):
    n_img, n_txt = cols * low, rows // low
    shard, width = images_ref.shape
    row, col = lax.axis_index("row"), lax.axis_index("col")
    high, below = lax.div(row, low), lax.rem(row, low)
    g_img = below * cols + col
    g_txt = high

    loads = [
        pltpu.make_async_copy(texts_ref, texts_at, load.at[0]),
        pltpu.make_async_copy(images_ref, images_at, load.at[1]),
    ]
    for item in loads:
        item.start()

    img_peers, txt_peers = [], []
    for step in range(1, n_txt):
        slot = paired(g_txt, step, n_txt)
        txt_peers.append((slot, (slot * low + below, col)))
    def img_device(slot):
        return high * low + lax.div(slot, cols), lax.rem(slot, cols)

    def sibling(slot):
        return slot + 1 - 2 * lax.rem(slot, 2)

    for step in range(1, n_img):
        slot = 2 * paired(lax.div(g_img, 2), step // 2, n_img // 2) + lax.rem(g_img + step, 2)
        img_peers.append((slot, img_device(slot)))
    same_core, other_core = img_peers[1::2], img_peers[0::2]
    twin = other_core[0]

    barrier = pltpu.get_barrier_semaphore()
    for _, peer in txt_peers + img_peers:
        pl.semaphore_signal(barrier, inc=1, device_id=peer, device_id_type=MESH)

    m_img = n_img * shard

    def keep(both, slot, offset, x):
        hi, lo = split(x)
        at = pl.multiple_of(slot * shard, shard)
        both[pl.ds(at, shard), :] = hi
        both[pl.ds(offset + at, shard), :] = lo

    loads[0].wait()
    unit_txt, norm_txt = normalize(texts_at[...])
    txt_all[g_txt] = unit_txt
    loads[1].wait()
    unit_img, norm_img = normalize(images_at[...])
    img_all[g_img] = unit_img
    pl.semaphore_wait(barrier, n_img + n_txt - 2)

    def copy(src, dst, send, recv, peer):
        return pltpu.make_async_remote_copy(
            src_ref=src, dst_ref=dst, send_sem=send, recv_sem=recv, device_id=peer, device_id_type=MESH
        )

    def gather(buf, send, recv, me, peers):
        for slot, peer in peers:
            copy(buf.at[me], buf.at[me], send.at[slot], recv.at[me], peer).start()

    def scatter(src, dst, send, recv, me, peers):
        for slot, peer in peers:
            copy(src.at[slot], dst.at[me], send.at[slot], recv.at[me], peer).start()

    def arrive(dst, send, recv, slot, peer):
        copy(dst.at[slot], dst.at[slot], send.at[slot], recv.at[slot], peer).wait_recv()

    def drain(dst, send, recv, peers):
        for slot, peer in peers:
            arrive(dst, send, recv, slot, peer)

    def sent(src, send, recv, peers):
        for slot, peer in peers:
            copy(src.at[slot], src.at[slot], send.at[slot], recv.at[slot], peer).wait_send()

    gather(txt_all, send_txt, recv_txt, g_txt, txt_peers)
    gather(img_all, send_img, recv_img, g_img, [twin] + same_core)

    keep(img_both, g_img, m_img, unit_img)
    for slot, peer in same_core:
        arrive(img_all, send_img, recv_img, slot, peer)
        copy(img_all.at[slot], img_all.at[slot], send_img.at[sibling(slot)], recv_img.at[slot], twin[1]).start()
        keep(img_both, slot, m_img, img_all[slot])
    for slot, peer in other_core:
        arrive(img_all, send_img, recv_img, slot, peer)
        keep(img_both, slot, m_img, img_all[slot])

    def total(x):
        return jnp.sum(jnp.sum(x, axis=0, keepdims=True), axis=1, keepdims=True)

    def fold(x):
        return sum(
            x[r : r + 8, c : c + 128] for r in range(0, x.shape[0], 8) for c in range(0, x.shape[1], 128)
        )

    temp = jnp.exp(scale_ref[:, 0:1])
    shift = scale_ref[:, 1:2]
    his, los = ([part] for part in split(unit_txt))
    for slot, peer in txt_peers:
        arrive(txt_all, send_txt, recv_txt, slot, peer)
        hi, lo = split(txt_all[slot])
        his.append(hi)
        los.append(lo)
    m_txt = n_txt * shard
    txt_both = jnp.concatenate(his + los, axis=0)
    prod = dot(txt_both, img_both[...], (1, 1))
    near, far = prod[:m_txt], prod[m_txt:]
    sim = (near[:, :m_img] + far[:, m_img:]) + (near[:, m_img:] + far[:, :m_img])
    logit = temp * sim + shift
    at = lax.broadcasted_iota(jnp.int32, (m_txt, m_img), 0)
    match = at == lax.broadcasted_iota(jnp.int32, (m_txt, m_img), 1) - g_img * shard
    sign = jnp.where(match & (at < shard), 1.0, -1.0).astype(F32)
    margin = -sign * logit
    small = jnp.exp(-jnp.abs(margin))
    pair_grad = -sign * (jnp.where(margin >= 0, 1.0, small) / (1.0 + small))
    g_hi, g_lo = split(temp * pair_grad)
    g_both = jnp.concatenate([g_hi, g_lo], axis=0)
    pt = dot(jnp.concatenate([g_both, g_both], axis=1), img_both[...], (1, 0))
    pt = pt[:m_txt] + pt[m_txt:]
    for at, slot in enumerate([g_txt] + [slot for slot, _ in txt_peers]):
        txt_part[slot] = pt[at * shard : (at + 1) * shard]
    scatter(txt_part, txt_recv, send_ptxt, recv_ptxt, g_txt, txt_peers[::-1])

    terms = (jnp.maximum(margin, 0.0) + jnp.log1p(small), pair_grad * sim, pair_grad)
    sums_img[g_img] = jnp.concatenate([fold(x) for x in terms], axis=0)
    gather(sums_img, send_s1, recv_s1, g_img, img_peers)
    pi = dot(
        jnp.concatenate([g_hi, g_hi, g_lo, g_lo], axis=0),
        jnp.concatenate([txt_both, txt_both], axis=0),
        (0, 0),
    )
    img_part[...] = pi.reshape(n_img, shard, width)
    scatter(img_part, img_recv, send_pimg, recv_pimg, g_img, img_peers[::-1])

    drain(sums_img, send_s1, recv_s1, img_peers)
    sums_txt[g_txt] = jnp.sum(sums_img[...], axis=0)
    gather(sums_txt, send_s2, recv_s2, g_txt, txt_peers)
    sent(txt_all, send_txt, recv_txt, txt_peers)
    sent(img_all, send_img, recv_img, img_peers)
    sent(sums_img, send_s1, recv_s1, img_peers)

    grad_txt = txt_part[g_txt]
    for slot, peer in txt_peers:
        arrive(txt_recv, send_ptxt, recv_ptxt, slot, peer)
        grad_txt = grad_txt + txt_recv[slot]
    grad_txt_ref[...] = unnormalize(unit_txt, norm_txt, grad_txt)
    grad_img = img_part[g_img]
    for slot, peer in img_peers:
        arrive(img_recv, send_pimg, recv_pimg, slot, peer)
        grad_img = grad_img + img_recv[slot]
    grad_img_ref[...] = unnormalize(unit_img, norm_img, grad_img)

    drain(sums_txt, send_s2, recv_s2, txt_peers)
    count = float(rows * cols * shard)
    final = jnp.sum(sums_txt[...], axis=0) / count
    loss, d_temp, d_bias = (total(final[at : at + 8]) for at in (0, 8, 16))
    lane = lax.broadcasted_iota(jnp.int32, (8, 128), 1)
    scalars_ref[...] = jnp.where(lane == 0, loss, jnp.where(lane == 1, temp * d_temp, d_bias))

    sent(txt_part, send_ptxt, recv_ptxt, txt_peers)
    sent(img_part, send_pimg, recv_pimg, img_peers)
    sent(sums_txt, send_s2, recv_s2, txt_peers)


def write_out(grad_img_ref, grad_txt_ref, scalars_ref, loss_ref, d_temp_ref, d_bias_ref, img_ref, txt_ref, parts, sem):
    writes = [
        pltpu.make_async_copy(grad_img_ref, img_ref, sem.at[0]),
        pltpu.make_async_copy(grad_txt_ref, txt_ref, sem.at[1]),
    ]
    for at, ref in enumerate((loss_ref, d_temp_ref, d_bias_ref)):
        parts[at] = scalars_ref[0:1, at : at + 1]
        writes.append(pltpu.make_async_copy(parts.at[at], ref, sem.at[2 + at]))
    for item in writes:
        item.start()
    for item in writes:
        item.wait()


def per_device(rows, cols, low, images, texts, log_temp, bias):
    shard, width = images.shape
    n_img, n_txt = cols * low, rows // low
    block = (shard, width)
    img_blocks, txt_blocks = pltpu.VMEM((n_img, *block), F32), pltpu.VMEM((n_txt, *block), F32)
    img_sems, txt_sems = pltpu.SemaphoreType.DMA((n_img,)), pltpu.SemaphoreType.DMA((n_txt,))
    vmem, hbm = pl.BlockSpec(memory_space=pltpu.VMEM), pl.BlockSpec(memory_space=pltpu.HBM)
    images, texts = (pltpu.with_memory_space_constraint(x, pltpu.HBM) for x in (images, texts))
    both = jnp.where(lax.broadcasted_iota(jnp.int32, (1, 128), 1) == 0, log_temp[0], bias[0])
    grad_img, grad_txt, scalars = pl.pallas_call(
        functools.partial(kernel, rows, cols, low),
        out_shape=[
            pltpu.VMEM(block, F32),
            pltpu.VMEM(block, F32),
            pltpu.VMEM((8, 128), F32),
        ],
        in_specs=[vmem, hbm, hbm],
        out_specs=[vmem, vmem, vmem],
        scratch_shapes=[
            pltpu.VMEM(block, F32), pltpu.VMEM(block, F32),
            pltpu.VMEM((2 * n_img * shard, width), BF16),
            img_blocks, txt_blocks, img_blocks, txt_blocks, img_blocks, txt_blocks,
            pltpu.VMEM((n_img, 24, 128), F32), pltpu.VMEM((n_txt, 24, 128), F32),
            img_sems, img_sems, txt_sems, txt_sems, img_sems, img_sems, txt_sems, txt_sems,
            img_sems, img_sems, txt_sems, txt_sems, pltpu.SemaphoreType.DMA((2,)),
        ],
        compiler_params=pltpu.CompilerParams(
            collective_id=0, has_side_effects=True, vmem_limit_bytes=48 * 1024 * 1024
        ),
        name="sigmoid_loss",
    )(both, images, texts)
    one = jax.ShapeDtypeStruct((1, 1), F32)
    held = (pltpu.with_memory_space_constraint(x, pltpu.VMEM) for x in (grad_img, grad_txt, scalars))
    loss, d_temp, d_bias, grad_img, grad_txt = pl.pallas_call(
        write_out,
        out_shape=[one, one, one, jax.ShapeDtypeStruct(block, F32), jax.ShapeDtypeStruct(block, F32)],
        in_specs=[vmem, vmem, vmem],
        out_specs=[hbm] * 5,
        scratch_shapes=[pltpu.VMEM((3, 1, 1), F32), pltpu.SemaphoreType.DMA((5,))],
        name="write_out",
    )(*held)
    return loss.reshape(1), d_temp.reshape(1), d_bias.reshape(1), grad_img, grad_txt


def solution(mesh):
    rows, cols = mesh.shape["row"], mesh.shape["col"]
    low = 1
    while cols * low < rows // low and rows % (2 * low) == 0:
        low *= 2
    in_specs = (P(("row", "col"), None), P(("row", "col"), None), P(), P())
    out_specs = (P(), P(), P(), P(("row", "col"), None), P(("row", "col"), None))
    return jax.shard_map(
        functools.partial(per_device, rows, cols, low),
        mesh=mesh, in_specs=in_specs, out_specs=out_specs, check_vma=False,
    )
```

```python
import functools

import jax
import jax.numpy as jnp
from jax import lax
from jax.experimental import pallas as pl
from jax.experimental.pallas import tpu as pltpu
from jax.sharding import PartitionSpec as P

MESH = pl.DeviceIdType.MESH
BF16 = jnp.bfloat16
F32 = jnp.float32


def split(x):
    hi = x.astype(BF16)
    return hi, (x - hi.astype(F32)).astype(BF16)


def dot(a, b, contract):
    return lax.dot_general(a, b, ((contract[:1], contract[1:]), ((), ())), preferred_element_type=F32)


def paired(slot, step, count):
    if count & (count - 1):
        return lax.rem(slot + step, count)
    bit = 1
    while bit < count:
        if step & bit:
            slot = slot + bit - 2 * bit * lax.rem(lax.div(slot, bit), 2)
        bit *= 2
    return slot


def normalize(x):
    norm = jnp.sqrt(jnp.sum(x * x, axis=1, keepdims=True) + 1e-06)
    return x / norm, norm


def unnormalize(unit, norm, grad_unit):
    inner = jnp.sum(unit * grad_unit, axis=1, keepdims=True)
    return (grad_unit - unit * inner) / norm


def kernel(
    rows, cols, low,
    scale_ref, images_ref, texts_ref,
    grad_img_ref, grad_txt_ref, scalars_ref,
    images_at, texts_at, img_both,
    img_all, txt_all, img_part, txt_part, img_recv, txt_recv, sums_img, sums_txt,
    send_img, recv_img, send_txt, recv_txt, send_pimg, recv_pimg, send_ptxt, recv_ptxt,
    send_s1, recv_s1, send_s2, recv_s2, load,
):
    n_img, n_txt = cols * low, rows // low
    shard, width = images_ref.shape
    row, col = lax.axis_index("row"), lax.axis_index("col")
    high, below = lax.div(row, low), lax.rem(row, low)
    g_img = below * cols + col
    g_txt = high

    loads = [
        pltpu.make_async_copy(texts_ref, texts_at, load.at[0]),
        pltpu.make_async_copy(images_ref, images_at, load.at[1]),
    ]
    for item in loads:
        item.start()

    img_peers, txt_peers = [], []
    for step in range(1, n_txt):
        slot = paired(g_txt, step, n_txt)
        txt_peers.append((slot, (slot * low + below, col)))
    def img_device(slot):
        return high * low + lax.div(slot, cols), lax.rem(slot, cols)

    for step in range(1, n_img):
        slot = 2 * paired(lax.div(g_img, 2), step // 2, n_img // 2) + lax.rem(g_img + step, 2)
        img_peers.append((slot, img_device(slot)))

    barrier = pltpu.get_barrier_semaphore()
    for _, peer in txt_peers + img_peers:
        pl.semaphore_signal(barrier, inc=1, device_id=peer, device_id_type=MESH)

    m_img = n_img * shard

    def keep(both, slot, offset, x):
        hi, lo = split(x)
        at = pl.multiple_of(slot * shard, shard)
        both[pl.ds(at, shard), :] = hi
        both[pl.ds(offset + at, shard), :] = lo

    loads[0].wait()
    unit_txt, norm_txt = normalize(texts_at[...])
    txt_all[g_txt] = unit_txt
    loads[1].wait()
    unit_img, norm_img = normalize(images_at[...])
    img_all[g_img] = unit_img
    pl.semaphore_wait(barrier, n_img + n_txt - 2)

    def copy(src, dst, send, recv, peer):
        return pltpu.make_async_remote_copy(
            src_ref=src, dst_ref=dst, send_sem=send, recv_sem=recv, device_id=peer, device_id_type=MESH
        )

    def gather(buf, send, recv, me, peers):
        for slot, peer in peers:
            copy(buf.at[me], buf.at[me], send.at[slot], recv.at[me], peer).start()

    def scatter(src, dst, send, recv, me, peers):
        for slot, peer in peers:
            copy(src.at[slot], dst.at[me], send.at[slot], recv.at[me], peer).start()

    def arrive(dst, send, recv, slot, peer):
        copy(dst.at[slot], dst.at[slot], send.at[slot], recv.at[slot], peer).wait_recv()

    def drain(dst, send, recv, peers):
        for slot, peer in peers:
            arrive(dst, send, recv, slot, peer)

    def sent(src, send, recv, peers):
        for slot, peer in peers:
            copy(src.at[slot], src.at[slot], send.at[slot], recv.at[slot], peer).wait_send()

    gather(txt_all, send_txt, recv_txt, g_txt, txt_peers)
    gather(img_all, send_img, recv_img, g_img, img_peers)

    keep(img_both, g_img, m_img, unit_img)
    for slot, peer in img_peers:
        arrive(img_all, send_img, recv_img, slot, peer)
        keep(img_both, slot, m_img, img_all[slot])

    def total(x):
        return jnp.sum(jnp.sum(x, axis=0, keepdims=True), axis=1, keepdims=True)

    temp = jnp.exp(scale_ref[:, 0:1])
    shift = scale_ref[:, 1:2]
    order = [(g_txt, None)] + txt_peers
    half = max(1, n_txt // 2)
    his, los, grads_hi, grads_lo = [], [], [], []
    loss_sum = temp_sum = bias_sum = 0.0
    for first in range(0, n_txt, half):
        group = order[first : first + half]
        rows_here = len(group) * shard
        for slot, peer in group:
            if peer is not None:
                arrive(txt_all, send_txt, recv_txt, slot, peer)
        txt_hi, txt_lo = split(jnp.concatenate([txt_all[slot] for slot, _ in group], axis=0))
        prod = dot(jnp.concatenate([txt_hi, txt_lo], axis=0), img_both[...], (1, 1))
        near, far = prod[:rows_here], prod[rows_here:]
        sim = (near[:, :m_img] + far[:, m_img:]) + (near[:, m_img:] + far[:, :m_img])
        logit = temp * sim + shift
        sign = -1.0
        if first == 0:
            at = lax.broadcasted_iota(jnp.int32, (rows_here, m_img), 0)
            match = at == lax.broadcasted_iota(jnp.int32, (rows_here, m_img), 1) - g_img * shard
            sign = jnp.where(match & (at < shard), 1.0, -1.0).astype(F32)
        margin = -sign * logit
        small = jnp.exp(-jnp.abs(margin))
        pair_grad = -sign * (jnp.where(margin >= 0, 1.0, small) / (1.0 + small))
        g_hi, g_lo = split(temp * pair_grad)
        g_both = jnp.concatenate([g_hi, g_lo], axis=0)
        pt = dot(jnp.concatenate([g_both, g_both], axis=1), img_both[...], (1, 0))
        pt = pt[:rows_here] + pt[rows_here:]
        for at, (slot, peer) in enumerate(group):
            txt_part[slot] = pt[at * shard : (at + 1) * shard]
        scatter(txt_part, txt_recv, send_ptxt, recv_ptxt, g_txt, [item for item in group if item[1] is not None])
        loss_sum += total(jnp.maximum(margin, 0.0) + jnp.log1p(small))
        temp_sum += total(pair_grad * sim)
        bias_sum += total(pair_grad)
        his.append(txt_hi)
        los.append(txt_lo)
        grads_hi.append(g_hi)
        grads_lo.append(g_lo)

    lane = lax.broadcasted_iota(jnp.int32, (8, 128), 1)
    part = jnp.where(lane == 0, loss_sum, jnp.where(lane == 1, temp_sum, bias_sum))
    sums_img[g_img] = part
    gather(sums_img, send_s1, recv_s1, g_img, img_peers)
    pi = dot(
        jnp.concatenate((grads_hi + grads_lo) * 2, axis=0),
        jnp.concatenate(his * 2 + los * 2, axis=0),
        (0, 0),
    )
    img_part[...] = pi.reshape(n_img, shard, width)
    scatter(img_part, img_recv, send_pimg, recv_pimg, g_img, img_peers)

    drain(sums_img, send_s1, recv_s1, img_peers)
    sums_txt[g_txt] = jnp.sum(sums_img[...], axis=0)
    gather(sums_txt, send_s2, recv_s2, g_txt, txt_peers)
    sent(txt_all, send_txt, recv_txt, txt_peers)
    sent(img_all, send_img, recv_img, img_peers)
    sent(sums_img, send_s1, recv_s1, img_peers)

    grad_txt = txt_part[g_txt]
    for slot, peer in txt_peers:
        arrive(txt_recv, send_ptxt, recv_ptxt, slot, peer)
        grad_txt = grad_txt + txt_recv[slot]
    grad_txt_ref[...] = unnormalize(unit_txt, norm_txt, grad_txt)
    grad_img = img_part[g_img]
    for slot, peer in img_peers:
        arrive(img_recv, send_pimg, recv_pimg, slot, peer)
        grad_img = grad_img + img_recv[slot]
    grad_img_ref[...] = unnormalize(unit_img, norm_img, grad_img)

    drain(sums_txt, send_s2, recv_s2, txt_peers)
    count = float(rows * cols * shard)
    final = jnp.sum(sums_txt[...], axis=0) / count
    scalars_ref[...] = jnp.where(lane == 1, temp * final, final)

    sent(txt_part, send_ptxt, recv_ptxt, txt_peers)
    sent(img_part, send_pimg, recv_pimg, img_peers)
    sent(sums_txt, send_s2, recv_s2, txt_peers)


def write_out(grad_img_ref, grad_txt_ref, scalars_ref, loss_ref, d_temp_ref, d_bias_ref, img_ref, txt_ref, parts, sem):
    writes = [
        pltpu.make_async_copy(grad_img_ref, img_ref, sem.at[0]),
        pltpu.make_async_copy(grad_txt_ref, txt_ref, sem.at[1]),
    ]
    for at, ref in enumerate((loss_ref, d_temp_ref, d_bias_ref)):
        parts[at] = scalars_ref[0:1, at : at + 1]
        writes.append(pltpu.make_async_copy(parts.at[at], ref, sem.at[2 + at]))
    for item in writes:
        item.start()
    for item in writes:
        item.wait()


def per_device(rows, cols, low, images, texts, log_temp, bias):
    shard, width = images.shape
    n_img, n_txt = cols * low, rows // low
    block = (shard, width)
    img_blocks, txt_blocks = pltpu.VMEM((n_img, *block), F32), pltpu.VMEM((n_txt, *block), F32)
    img_sems, txt_sems = pltpu.SemaphoreType.DMA((n_img,)), pltpu.SemaphoreType.DMA((n_txt,))
    vmem, hbm = pl.BlockSpec(memory_space=pltpu.VMEM), pl.BlockSpec(memory_space=pltpu.HBM)
    images, texts = (pltpu.with_memory_space_constraint(x, pltpu.HBM) for x in (images, texts))
    both = jnp.where(lax.broadcasted_iota(jnp.int32, (1, 128), 1) == 0, log_temp[0], bias[0])
    grad_img, grad_txt, scalars = pl.pallas_call(
        functools.partial(kernel, rows, cols, low),
        out_shape=[
            pltpu.VMEM(block, F32),
            pltpu.VMEM(block, F32),
            pltpu.VMEM((8, 128), F32),
        ],
        in_specs=[vmem, hbm, hbm],
        out_specs=[vmem, vmem, vmem],
        scratch_shapes=[
            pltpu.VMEM(block, F32), pltpu.VMEM(block, F32),
            pltpu.VMEM((2 * n_img * shard, width), BF16),
            img_blocks, txt_blocks, img_blocks, txt_blocks, img_blocks, txt_blocks,
            pltpu.VMEM((n_img, 8, 128), F32), pltpu.VMEM((n_txt, 8, 128), F32),
            img_sems, img_sems, txt_sems, txt_sems, img_sems, img_sems, txt_sems, txt_sems,
            img_sems, img_sems, txt_sems, txt_sems, pltpu.SemaphoreType.DMA((2,)),
        ],
        compiler_params=pltpu.CompilerParams(
            collective_id=0, has_side_effects=True, vmem_limit_bytes=48 * 1024 * 1024
        ),
        name="sigmoid_loss",
    )(both, images, texts)
    one = jax.ShapeDtypeStruct((1, 1), F32)
    held = (pltpu.with_memory_space_constraint(x, pltpu.VMEM) for x in (grad_img, grad_txt, scalars))
    loss, d_temp, d_bias, grad_img, grad_txt = pl.pallas_call(
        write_out,
        out_shape=[one, one, one, jax.ShapeDtypeStruct(block, F32), jax.ShapeDtypeStruct(block, F32)],
        in_specs=[vmem, vmem, vmem],
        out_specs=[hbm] * 5,
        scratch_shapes=[pltpu.VMEM((3, 1, 1), F32), pltpu.SemaphoreType.DMA((5,))],
        name="write_out",
    )(*held)
    return loss.reshape(1), d_temp.reshape(1), d_bias.reshape(1), grad_img, grad_txt


def solution(mesh):
    rows, cols = mesh.shape["row"], mesh.shape["col"]
    low = 1
    while cols * low < rows // low and rows % (2 * low) == 0:
        low *= 2
    in_specs = (P(("row", "col"), None), P(("row", "col"), None), P(), P())
    out_specs = (P(), P(), P(), P(("row", "col"), None), P(("row", "col"), None))
    return jax.shard_map(
        functools.partial(per_device, rows, cols, low),
        mesh=mesh, in_specs=in_specs, out_specs=out_specs, check_vma=False,
    )
```

```python
import functools

import jax
import jax.numpy as jnp
from jax import lax
from jax.experimental import pallas as pl
from jax.experimental.pallas import tpu as pltpu
from jax.sharding import PartitionSpec as P

MESH = pl.DeviceIdType.MESH
BF16 = jnp.bfloat16
F32 = jnp.float32


def split(x):
    hi = x.astype(BF16)
    return hi, (x - hi.astype(F32)).astype(BF16)


def dot(a, b, contract):
    return lax.dot_general(a, b, ((contract[:1], contract[1:]), ((), ())), preferred_element_type=F32)


def normalize(x):
    norm = jnp.sqrt(jnp.sum(x * x, axis=1, keepdims=True) + 1e-06)
    return x / norm, norm


def unnormalize(unit, norm, grad_unit):
    inner = jnp.sum(unit * grad_unit, axis=1, keepdims=True)
    return (grad_unit - unit * inner) / norm


def kernel(
    rows, cols, low,
    scale_ref, images_ref, texts_ref,
    grad_img_ref, grad_txt_ref, scalars_ref,
    images_at, texts_at, img_both,
    img_all, txt_all, img_part, txt_part, img_recv, txt_recv, sums_img, sums_txt,
    send_img, recv_img, send_txt, recv_txt, send_pimg, recv_pimg, send_ptxt, recv_ptxt,
    send_s1, recv_s1, send_s2, recv_s2, load,
):
    n_img, n_txt = cols * low, rows // low
    shard, width = images_ref.shape
    row, col = lax.axis_index("row"), lax.axis_index("col")
    high, below = lax.div(row, low), lax.rem(row, low)
    g_img = below * cols + col
    g_txt = high

    loads = [
        pltpu.make_async_copy(texts_ref, texts_at, load.at[0]),
        pltpu.make_async_copy(images_ref, images_at, load.at[1]),
    ]
    for item in loads:
        item.start()

    img_peers, txt_peers = [], []
    for step in range(1, n_txt):
        slot = lax.rem(g_txt + step, n_txt)
        txt_peers.append((slot, (slot * low + below, col)))
    def img_device(slot):
        return high * low + lax.div(slot, cols), lax.rem(slot, cols)

    def sibling(slot):
        return slot + 1 - 2 * lax.rem(slot, 2)

    for step in range(1, n_img):
        slot = 2 * lax.rem(lax.div(g_img, 2) + step // 2, n_img // 2) + lax.rem(g_img + step, 2)
        img_peers.append((slot, img_device(slot)))
    same_core, other_core = img_peers[1::2], img_peers[0::2]
    twin = other_core[0]

    barrier = pltpu.get_barrier_semaphore()
    for _, peer in txt_peers + img_peers:
        pl.semaphore_signal(barrier, inc=1, device_id=peer, device_id_type=MESH)

    m_img = n_img * shard

    def keep(both, slot, offset, x):
        hi, lo = split(x)
        at = pl.multiple_of(slot * shard, shard)
        both[pl.ds(at, shard), :] = hi
        both[pl.ds(offset + at, shard), :] = lo

    loads[0].wait()
    unit_txt, norm_txt = normalize(texts_at[...])
    txt_all[g_txt] = unit_txt
    loads[1].wait()
    unit_img, norm_img = normalize(images_at[...])
    img_all[g_img] = unit_img
    pl.semaphore_wait(barrier, n_img + n_txt - 2)

    def copy(src, dst, send, recv, peer):
        return pltpu.make_async_remote_copy(
            src_ref=src, dst_ref=dst, send_sem=send, recv_sem=recv, device_id=peer, device_id_type=MESH
        )

    def gather(buf, send, recv, me, peers):
        for slot, peer in peers:
            copy(buf.at[me], buf.at[me], send.at[slot], recv.at[me], peer).start()

    def scatter(src, dst, send, recv, me, peers):
        for slot, peer in peers:
            copy(src.at[slot], dst.at[me], send.at[slot], recv.at[me], peer).start()

    def arrive(dst, send, recv, slot, peer):
        copy(dst.at[slot], dst.at[slot], send.at[slot], recv.at[slot], peer).wait_recv()

    def drain(dst, send, recv, peers):
        for slot, peer in peers:
            arrive(dst, send, recv, slot, peer)

    def sent(src, send, recv, peers):
        for slot, peer in peers:
            copy(src.at[slot], src.at[slot], send.at[slot], recv.at[slot], peer).wait_send()

    gather(txt_all, send_txt, recv_txt, g_txt, txt_peers)
    gather(img_all, send_img, recv_img, g_img, [twin] + same_core)

    keep(img_both, g_img, m_img, unit_img)
    for slot, peer in same_core:
        arrive(img_all, send_img, recv_img, slot, peer)
        copy(img_all.at[slot], img_all.at[slot], send_img.at[sibling(slot)], recv_img.at[slot], twin[1]).start()
        keep(img_both, slot, m_img, img_all[slot])
    for slot, peer in other_core:
        arrive(img_all, send_img, recv_img, slot, peer)
        keep(img_both, slot, m_img, img_all[slot])

    def total(x):
        return jnp.sum(jnp.sum(x, axis=0, keepdims=True), axis=1, keepdims=True)

    temp = jnp.exp(scale_ref[:, 0:1])
    shift = scale_ref[:, 1:2]
    order = [(g_txt, None)] + txt_peers
    half = max(1, n_txt // 2)
    his, los, grads_hi, grads_lo = [], [], [], []
    loss_sum = temp_sum = bias_sum = 0.0
    for first in range(0, n_txt, half):
        group = order[first : first + half]
        rows_here = len(group) * shard
        for slot, peer in group:
            if peer is not None:
                arrive(txt_all, send_txt, recv_txt, slot, peer)
        txt_hi, txt_lo = split(jnp.concatenate([txt_all[slot] for slot, _ in group], axis=0))
        prod = dot(jnp.concatenate([txt_hi, txt_lo], axis=0), img_both[...], (1, 1))
        near, far = prod[:rows_here], prod[rows_here:]
        sim = (near[:, :m_img] + far[:, m_img:]) + (near[:, m_img:] + far[:, :m_img])
        logit = temp * sim + shift
        sign = -1.0
        if first == 0:
            at = lax.broadcasted_iota(jnp.int32, (rows_here, m_img), 0)
            match = at == lax.broadcasted_iota(jnp.int32, (rows_here, m_img), 1) - g_img * shard
            sign = jnp.where(match & (at < shard), 1.0, -1.0).astype(F32)
        margin = -sign * logit
        small = jnp.exp(-jnp.abs(margin))
        pair_grad = -sign * (jnp.where(margin >= 0, 1.0, small) / (1.0 + small))
        g_hi, g_lo = split(temp * pair_grad)
        g_both = jnp.concatenate([g_hi, g_lo], axis=0)
        pt = dot(jnp.concatenate([g_both, g_both], axis=1), img_both[...], (1, 0))
        pt = pt[:rows_here] + pt[rows_here:]
        for at, (slot, peer) in enumerate(group):
            txt_part[slot] = pt[at * shard : (at + 1) * shard]
        scatter(txt_part, txt_recv, send_ptxt, recv_ptxt, g_txt, [item for item in group if item[1] is not None])
        loss_sum += total(jnp.maximum(margin, 0.0) + jnp.log1p(small))
        temp_sum += total(pair_grad * sim)
        bias_sum += total(pair_grad)
        his.append(txt_hi)
        los.append(txt_lo)
        grads_hi.append(g_hi)
        grads_lo.append(g_lo)

    lane = lax.broadcasted_iota(jnp.int32, (8, 128), 1)
    part = jnp.where(lane == 0, loss_sum, jnp.where(lane == 1, temp_sum, bias_sum))
    sums_img[g_img] = part
    gather(sums_img, send_s1, recv_s1, g_img, img_peers)
    pi = dot(
        jnp.concatenate((grads_hi + grads_lo) * 2, axis=0),
        jnp.concatenate(his * 2 + los * 2, axis=0),
        (0, 0),
    )
    img_part[...] = pi.reshape(n_img, shard, width)
    scatter(img_part, img_recv, send_pimg, recv_pimg, g_img, img_peers)

    drain(sums_img, send_s1, recv_s1, img_peers)
    sums_txt[g_txt] = jnp.sum(sums_img[...], axis=0)
    gather(sums_txt, send_s2, recv_s2, g_txt, txt_peers)
    sent(txt_all, send_txt, recv_txt, txt_peers)
    sent(img_all, send_img, recv_img, img_peers)
    sent(sums_img, send_s1, recv_s1, img_peers)

    grad_txt = txt_part[g_txt]
    for slot, peer in txt_peers:
        arrive(txt_recv, send_ptxt, recv_ptxt, slot, peer)
        grad_txt = grad_txt + txt_recv[slot]
    grad_txt_ref[...] = unnormalize(unit_txt, norm_txt, grad_txt)
    grad_img = img_part[g_img]
    for slot, peer in img_peers:
        arrive(img_recv, send_pimg, recv_pimg, slot, peer)
        grad_img = grad_img + img_recv[slot]
    grad_img_ref[...] = unnormalize(unit_img, norm_img, grad_img)

    drain(sums_txt, send_s2, recv_s2, txt_peers)
    count = float(rows * cols * shard)
    final = jnp.sum(sums_txt[...], axis=0) / count
    scalars_ref[...] = jnp.where(lane == 1, temp * final, final)

    sent(txt_part, send_ptxt, recv_ptxt, txt_peers)
    sent(img_part, send_pimg, recv_pimg, img_peers)
    sent(sums_txt, send_s2, recv_s2, txt_peers)


def write_out(grad_img_ref, grad_txt_ref, scalars_ref, loss_ref, d_temp_ref, d_bias_ref, img_ref, txt_ref, parts, sem):
    writes = [
        pltpu.make_async_copy(grad_img_ref, img_ref, sem.at[0]),
        pltpu.make_async_copy(grad_txt_ref, txt_ref, sem.at[1]),
    ]
    for at, ref in enumerate((loss_ref, d_temp_ref, d_bias_ref)):
        parts[at] = scalars_ref[0:1, at : at + 1]
        writes.append(pltpu.make_async_copy(parts.at[at], ref, sem.at[2 + at]))
    for item in writes:
        item.start()
    for item in writes:
        item.wait()


def per_device(rows, cols, low, images, texts, log_temp, bias):
    shard, width = images.shape
    n_img, n_txt = cols * low, rows // low
    block = (shard, width)
    img_blocks, txt_blocks = pltpu.VMEM((n_img, *block), F32), pltpu.VMEM((n_txt, *block), F32)
    img_sems, txt_sems = pltpu.SemaphoreType.DMA((n_img,)), pltpu.SemaphoreType.DMA((n_txt,))
    vmem, hbm = pl.BlockSpec(memory_space=pltpu.VMEM), pl.BlockSpec(memory_space=pltpu.HBM)
    images, texts = (pltpu.with_memory_space_constraint(x, pltpu.HBM) for x in (images, texts))
    both = jnp.where(lax.broadcasted_iota(jnp.int32, (1, 128), 1) == 0, log_temp[0], bias[0])
    grad_img, grad_txt, scalars = pl.pallas_call(
        functools.partial(kernel, rows, cols, low),
        out_shape=[
            pltpu.VMEM(block, F32),
            pltpu.VMEM(block, F32),
            pltpu.VMEM((8, 128), F32),
        ],
        in_specs=[vmem, hbm, hbm],
        out_specs=[vmem, vmem, vmem],
        scratch_shapes=[
            pltpu.VMEM(block, F32), pltpu.VMEM(block, F32),
            pltpu.VMEM((2 * n_img * shard, width), BF16),
            img_blocks, txt_blocks, img_blocks, txt_blocks, img_blocks, txt_blocks,
            pltpu.VMEM((n_img, 8, 128), F32), pltpu.VMEM((n_txt, 8, 128), F32),
            img_sems, img_sems, txt_sems, txt_sems, img_sems, img_sems, txt_sems, txt_sems,
            img_sems, img_sems, txt_sems, txt_sems, pltpu.SemaphoreType.DMA((2,)),
        ],
        compiler_params=pltpu.CompilerParams(
            collective_id=0, has_side_effects=True, vmem_limit_bytes=48 * 1024 * 1024
        ),
        name="sigmoid_loss",
    )(both, images, texts)
    one = jax.ShapeDtypeStruct((1, 1), F32)
    held = (pltpu.with_memory_space_constraint(x, pltpu.VMEM) for x in (grad_img, grad_txt, scalars))
    loss, d_temp, d_bias, grad_img, grad_txt = pl.pallas_call(
        write_out,
        out_shape=[one, one, one, jax.ShapeDtypeStruct(block, F32), jax.ShapeDtypeStruct(block, F32)],
        in_specs=[vmem, vmem, vmem],
        out_specs=[hbm] * 5,
        scratch_shapes=[pltpu.VMEM((3, 1, 1), F32), pltpu.SemaphoreType.DMA((5,))],
        name="write_out",
    )(*held)
    return loss.reshape(1), d_temp.reshape(1), d_bias.reshape(1), grad_img, grad_txt


def solution(mesh):
    rows, cols = mesh.shape["row"], mesh.shape["col"]
    low = 1
    while cols * low < rows // low and rows % (2 * low) == 0:
        low *= 2
    in_specs = (P(("row", "col"), None), P(("row", "col"), None), P(), P())
    out_specs = (P(), P(), P(), P(("row", "col"), None), P(("row", "col"), None))
    return jax.shard_map(
        functools.partial(per_device, rows, cols, low),
        mesh=mesh, in_specs=in_specs, out_specs=out_specs, check_vma=False,
    )
```

```python
import functools

import jax
import jax.numpy as jnp
from jax import lax
from jax.experimental import pallas as pl
from jax.experimental.pallas import tpu as pltpu
from jax.sharding import PartitionSpec as P

MESH = pl.DeviceIdType.MESH
BF16 = jnp.bfloat16
F32 = jnp.float32


def split(x):
    hi = x.astype(BF16)
    return hi, (x - hi.astype(F32)).astype(BF16)


def dot(a, b, contract):
    return lax.dot_general(a, b, ((contract[:1], contract[1:]), ((), ())), preferred_element_type=F32)


def normalize(x):
    norm = jnp.sqrt(jnp.sum(x * x, axis=1, keepdims=True) + 1e-06)
    return x / norm, norm


def unnormalize(unit, norm, grad_unit):
    inner = jnp.sum(unit * grad_unit, axis=1, keepdims=True)
    return (grad_unit - unit * inner) / norm


def kernel(
    rows, cols, low,
    log_temp_ref, bias_ref, images_ref, texts_ref,
    grad_img_ref, grad_txt_ref, scalars_ref,
    images_at, texts_at, img_both, txt_both,
    img_all, txt_all, img_part, txt_part, img_recv, txt_recv, sums_img, sums_txt,
    send_img, recv_img, send_txt, recv_txt, send_pimg, recv_pimg, send_ptxt, recv_ptxt,
    send_s1, recv_s1, send_s2, recv_s2, load,
):
    n_img, n_txt = cols * low, rows // low
    shard, width = images_ref.shape
    row, col = lax.axis_index("row"), lax.axis_index("col")
    high, below = lax.div(row, low), lax.rem(row, low)
    g_img = below * cols + col
    g_txt = high

    loads = [
        pltpu.make_async_copy(texts_ref, texts_at, load.at[0]),
        pltpu.make_async_copy(images_ref, images_at, load.at[1]),
    ]
    for item in loads:
        item.start()

    img_peers, txt_peers = [], []
    for step in range(1, n_txt):
        slot = lax.rem(g_txt + step, n_txt)
        txt_peers.append((slot, (slot * low + below, col)))
    def img_device(slot):
        return high * low + lax.div(slot, cols), lax.rem(slot, cols)

    def sibling(slot):
        return slot + 1 - 2 * lax.rem(slot, 2)

    for step in range(1, n_img):
        slot = 2 * lax.rem(lax.div(g_img, 2) + step // 2, n_img // 2) + lax.rem(g_img + step, 2)
        img_peers.append((slot, img_device(slot)))
    same_core, other_core = img_peers[1::2], img_peers[0::2]
    twin = other_core[0]

    barrier = pltpu.get_barrier_semaphore()
    for _, peer in txt_peers + img_peers:
        pl.semaphore_signal(barrier, inc=1, device_id=peer, device_id_type=MESH)

    m_txt, m_img = n_txt * shard, n_img * shard

    def keep(both, slot, offset, x):
        hi, lo = split(x)
        at = pl.multiple_of(slot * shard, shard)
        both[pl.ds(at, shard), :] = hi
        both[pl.ds(offset + at, shard), :] = lo

    loads[0].wait()
    unit_txt, norm_txt = normalize(texts_at[...])
    txt_all[g_txt] = unit_txt
    loads[1].wait()
    unit_img, norm_img = normalize(images_at[...])
    img_all[g_img] = unit_img
    pl.semaphore_wait(barrier, n_img + n_txt - 2)

    def copy(src, dst, send, recv, peer):
        return pltpu.make_async_remote_copy(
            src_ref=src, dst_ref=dst, send_sem=send, recv_sem=recv, device_id=peer, device_id_type=MESH
        )

    def gather(buf, send, recv, me, peers):
        for slot, peer in peers:
            copy(buf.at[me], buf.at[me], send.at[slot], recv.at[me], peer).start()

    def scatter(src, dst, send, recv, me, peers):
        for slot, peer in peers:
            copy(src.at[slot], dst.at[me], send.at[slot], recv.at[me], peer).start()

    def arrive(dst, send, recv, slot, peer):
        copy(dst.at[slot], dst.at[slot], send.at[slot], recv.at[slot], peer).wait_recv()

    def drain(dst, send, recv, peers):
        for slot, peer in peers:
            arrive(dst, send, recv, slot, peer)

    def sent(src, send, recv, peers):
        for slot, peer in peers:
            copy(src.at[slot], src.at[slot], send.at[slot], recv.at[slot], peer).wait_send()

    gather(txt_all, send_txt, recv_txt, g_txt, txt_peers)
    gather(img_all, send_img, recv_img, g_img, [twin] + same_core)

    keep(txt_both, g_txt, m_txt, unit_txt)
    keep(img_both, g_img, m_img, unit_img)
    temp = jnp.exp(jnp.full((1, 1), log_temp_ref[0], F32))
    shift = bias_ref[0]
    for slot, peer in same_core:
        arrive(img_all, send_img, recv_img, slot, peer)
        copy(img_all.at[slot], img_all.at[slot], send_img.at[sibling(slot)], recv_img.at[slot], twin[1]).start()
        keep(img_both, slot, m_img, img_all[slot])
    for slot, peer in other_core:
        arrive(img_all, send_img, recv_img, slot, peer)
        keep(img_both, slot, m_img, img_all[slot])
    for slot, peer in txt_peers:
        arrive(txt_all, send_txt, recv_txt, slot, peer)
        keep(txt_both, slot, m_txt, txt_all[slot])

    prod = dot(txt_both[...], img_both[...], (1, 1))
    sim = (prod[:m_txt, :m_img] + prod[m_txt:, m_img:]) + (prod[:m_txt, m_img:] + prod[m_txt:, :m_img])
    logit = temp * sim + shift
    at = lax.broadcasted_iota(jnp.int32, (m_txt, m_img), 0) - g_txt * shard
    diagonal = (at == lax.broadcasted_iota(jnp.int32, (m_txt, m_img), 1) - g_img * shard) & (at >= 0) & (at < shard)
    sign = jnp.where(diagonal, 1.0, -1.0).astype(F32)
    margin = -sign * logit
    small = jnp.exp(-jnp.abs(margin))
    pair_grad = -sign * (jnp.where(margin >= 0, 1.0, small) / (1.0 + small))

    def total(x):
        return jnp.sum(jnp.sum(x, axis=0, keepdims=True), axis=1, keepdims=True)

    g_hi, g_lo = split(temp * pair_grad)
    g_both = jnp.concatenate([g_hi, g_lo], axis=0)
    pt = dot(jnp.concatenate([g_both, g_both], axis=1), img_both[...], (1, 0))
    txt_part[...] = (pt[:m_txt] + pt[m_txt:]).reshape(n_txt, shard, width)
    scatter(txt_part, txt_recv, send_ptxt, recv_ptxt, g_txt, txt_peers)

    soft = jnp.maximum(margin, 0.0) + jnp.log1p(small)
    lane = lax.broadcasted_iota(jnp.int32, (8, 128), 1)
    part = jnp.where(lane == 0, total(soft), jnp.where(lane == 1, total(pair_grad * sim), total(pair_grad)))
    sums_img[g_img] = part
    gather(sums_img, send_s1, recv_s1, g_img, img_peers)

    pi = dot(
        jnp.concatenate([g_hi, g_hi, g_lo, g_lo], axis=0),
        jnp.concatenate([txt_both[...], txt_both[...]], axis=0),
        (0, 0),
    )
    img_part[...] = pi.reshape(n_img, shard, width)
    scatter(img_part, img_recv, send_pimg, recv_pimg, g_img, img_peers)

    drain(sums_img, send_s1, recv_s1, img_peers)
    sums_txt[g_txt] = jnp.sum(sums_img[...], axis=0)
    gather(sums_txt, send_s2, recv_s2, g_txt, txt_peers)
    sent(txt_all, send_txt, recv_txt, txt_peers)
    sent(img_all, send_img, recv_img, img_peers)
    sent(sums_img, send_s1, recv_s1, img_peers)

    grad_txt = txt_part[g_txt]
    for slot, peer in txt_peers:
        arrive(txt_recv, send_ptxt, recv_ptxt, slot, peer)
        grad_txt = grad_txt + txt_recv[slot]
    grad_txt_ref[...] = unnormalize(unit_txt, norm_txt, grad_txt)
    grad_img = img_part[g_img]
    for slot, peer in img_peers:
        arrive(img_recv, send_pimg, recv_pimg, slot, peer)
        grad_img = grad_img + img_recv[slot]
    grad_img_ref[...] = unnormalize(unit_img, norm_img, grad_img)

    drain(sums_txt, send_s2, recv_s2, txt_peers)
    count = float(rows * cols * shard)
    final = jnp.sum(sums_txt[...], axis=0) / count
    scalars_ref[...] = jnp.where(lane == 1, temp * final, final)

    sent(txt_part, send_ptxt, recv_ptxt, txt_peers)
    sent(img_part, send_pimg, recv_pimg, img_peers)
    sent(sums_txt, send_s2, recv_s2, txt_peers)


def write_out(grad_img_ref, grad_txt_ref, scalars_ref, loss_ref, d_temp_ref, d_bias_ref, img_ref, txt_ref, parts, sem):
    writes = [
        pltpu.make_async_copy(grad_img_ref, img_ref, sem.at[0]),
        pltpu.make_async_copy(grad_txt_ref, txt_ref, sem.at[1]),
    ]
    for at, ref in enumerate((loss_ref, d_temp_ref, d_bias_ref)):
        parts[at] = scalars_ref[0:1, at : at + 1]
        writes.append(pltpu.make_async_copy(parts.at[at], ref, sem.at[2 + at]))
    for item in writes:
        item.start()
    for item in writes:
        item.wait()


def per_device(rows, cols, low, images, texts, log_temp, bias):
    shard, width = images.shape
    n_img, n_txt = cols * low, rows // low
    block = (shard, width)
    img_blocks, txt_blocks = pltpu.VMEM((n_img, *block), F32), pltpu.VMEM((n_txt, *block), F32)
    img_sems, txt_sems = pltpu.SemaphoreType.DMA((n_img,)), pltpu.SemaphoreType.DMA((n_txt,))
    vmem, smem = pl.BlockSpec(memory_space=pltpu.VMEM), pl.BlockSpec(memory_space=pltpu.SMEM)
    hbm = pl.BlockSpec(memory_space=pltpu.HBM)
    images, texts = (pltpu.with_memory_space_constraint(x, pltpu.HBM) for x in (images, texts))
    grad_img, grad_txt, scalars = pl.pallas_call(
        functools.partial(kernel, rows, cols, low),
        out_shape=[
            pltpu.VMEM(block, F32),
            pltpu.VMEM(block, F32),
            pltpu.VMEM((8, 128), F32),
        ],
        in_specs=[smem, smem, hbm, hbm],
        out_specs=[vmem, vmem, vmem],
        scratch_shapes=[
            pltpu.VMEM(block, F32), pltpu.VMEM(block, F32),
            pltpu.VMEM((2 * n_img * shard, width), BF16), pltpu.VMEM((2 * n_txt * shard, width), BF16),
            img_blocks, txt_blocks, img_blocks, txt_blocks, img_blocks, txt_blocks,
            pltpu.VMEM((n_img, 8, 128), F32), pltpu.VMEM((n_txt, 8, 128), F32),
            img_sems, img_sems, txt_sems, txt_sems, img_sems, img_sems, txt_sems, txt_sems,
            img_sems, img_sems, txt_sems, txt_sems, pltpu.SemaphoreType.DMA((2,)),
        ],
        compiler_params=pltpu.CompilerParams(
            collective_id=0, has_side_effects=True, vmem_limit_bytes=48 * 1024 * 1024
        ),
        name="sigmoid_loss",
    )(log_temp, bias, images, texts)
    one = jax.ShapeDtypeStruct((1, 1), F32)
    held = (pltpu.with_memory_space_constraint(x, pltpu.VMEM) for x in (grad_img, grad_txt, scalars))
    loss, d_temp, d_bias, grad_img, grad_txt = pl.pallas_call(
        write_out,
        out_shape=[one, one, one, jax.ShapeDtypeStruct(block, F32), jax.ShapeDtypeStruct(block, F32)],
        in_specs=[vmem, vmem, vmem],
        out_specs=[hbm] * 5,
        scratch_shapes=[pltpu.VMEM((3, 1, 1), F32), pltpu.SemaphoreType.DMA((5,))],
        name="write_out",
    )(*held)
    return loss.reshape(1), d_temp.reshape(1), d_bias.reshape(1), grad_img, grad_txt


def solution(mesh):
    rows, cols = mesh.shape["row"], mesh.shape["col"]
    low = 1
    while cols * low < rows // low and rows % (2 * low) == 0:
        low *= 2
    in_specs = (P(("row", "col"), None), P(("row", "col"), None), P(), P())
    out_specs = (P(), P(), P(), P(("row", "col"), None), P(("row", "col"), None))
    return jax.shard_map(
        functools.partial(per_device, rows, cols, low),
        mesh=mesh, in_specs=in_specs, out_specs=out_specs, check_vma=False,
    )
```
